256 devices in a mesh: row: 32 (over z, y), col: 8 (over x, core).
Axes of the slice: x: 4, y: 4, z: 8, core: 2. Of those that a mesh axis runs over, the one named last changes fastest.
Arguments:
- tokens: bfloat16 [1024, 12288], P('row', 'col'), may hold values from -6 to 6
- w_in: bfloat16 [12288, 24576], P('col', 'row'), may hold values from -0.0546875 to 0.0546875
- bias_in: float32 [24576], P('row'), may hold values from -4 to 4
- w_out: bfloat16 [24576, 12288], P('row', 'col'), may hold values from -0.0390625 to 0.0390625
- bias_out: float32 [12288], P('col'), may hold values from -4 to 4
- cotangent: bfloat16 [1024, 12288], P('row', 'col'), may hold values from -6 to 6
Outputs:
- outputs: bfloat16 [1024, 12288], P('row', 'col')
- d_tokens: bfloat16 [1024, 12288], P('row', 'col')
- grad_w_in: bfloat16 [12288, 24576], P('col', 'row')
- grad_bias_in: float32 [24576], P('row')
- grad_w_out: bfloat16 [24576, 12288], P('row', 'col')
- grad_bias_out: float32 [12288], P('col')
The draws below stay inside these ranges and needn't reach their ends.
All inputs are finite; a program needn't handle non-finite values.
Results may differ from the reference program's by a relative error of at most 0.03.
Values may be sent and summed in bfloat16 or wider, within the bound.
A program may use at most 64 MiB of HBM per device.

```python
import math
import jax
import jax.numpy as jnp
from jax import lax

D = 12288
FFW = 24576
TOKENS = 1024
N_ROW = 32
N_COL = 8


def level_of(rng, extent, shards, smallest, largest):
    def one(axis_at, parts):
        heights = jax.random.uniform(jax.random.fold_in(jax.random.fold_in(rng, 6), axis_at), (parts,), jnp.float32, smallest / len(shards), largest / len(shards))
        return jnp.repeat(jnp.exp(heights), extent[axis_at] // parts).reshape((-1,) + (1,) * (len(extent) - axis_at - 1))

    gain = one(*shards[0])
    for cut in shards[1:]:
        gain = gain * one(*cut)
    return gain


def gaussian(own_key, dims, deviation, most, cuts=(), held_as=jnp.bfloat16):
    values = jax.random.normal(own_key, dims, jnp.float32) * deviation
    if len(cuts) > 0:
        values = level_of(own_key, dims, cuts, -0.22, 0.18) * values
    return jnp.clip(values, min=-most, max=most).astype(held_as)


def setup_inputs(seed: int = 0) -> dict:
    key_list = jax.random.split(jax.random.key(seed), 7)
    return {
        "tokens": gaussian(key_list[0], (TOKENS, D), 1.0, 6.0, ((0, 32), (1, 8))),
        "w_in": gaussian(key_list[1], (D, FFW), D ** -0.5, 0.0546875, ((0, 8), (1, 32))),
        "bias_in": gaussian(key_list[2], (FFW,), 1.0, 4.0, ((0, 32),), jnp.float32),
        "w_out": gaussian(key_list[3], (FFW, D), FFW ** -0.5, 0.0390625, ((0, 32), (1, 8))),
        "bias_out": gaussian(key_list[4], (D,), 1.0, 4.0, ((0, 8),), jnp.float32),
        "cotangent": gaussian(key_list[5], (TOKENS, D), 1.0, 6.0, ((0, 32), (1, 8))),
    }


gelu_coef = math.sqrt(2.0 / math.pi)

def gelu_pair(preact):
    inner = gelu_coef * (preact + 0.044715 * preact * preact * preact)
    tangent = jnp.tanh(inner)
    value = 0.5 * preact * (1.0 + tangent)
    slope = 0.5 * (1.0 + tangent) + 0.5 * preact * (1.0 - tangent * tangent) * gelu_coef * (1.0 + 3.0 * 0.044715 * preact * preact)
    return (value, slope)

def contract(left, right, left_dim, right_dim):
    return lax.dot_general(left, right, (((left_dim,), (right_dim,)), ((), ())), preferred_element_type=jnp.float32)

def block_sum(left, right, left_dim, right_dim, blocks):
    width = left.shape[left_dim] // blocks
    shape = (left.shape[1 - left_dim], right.shape[1 - right_dim])

    def step(total, index):
        start = (index * width).astype(jnp.int32)
        left_piece = lax.dynamic_slice_in_dim(left, start, width, left_dim)
        right_piece = lax.dynamic_slice_in_dim(right, start, width, right_dim)
        part = contract(left_piece, right_piece, left_dim, right_dim)
        rounded = lax.optimization_barrier(part.astype(jnp.bfloat16))
        return (total + rounded.astype(jnp.float32), None)
    total, unused = lax.scan(step, jnp.zeros(shape, jnp.float32), jnp.arange(blocks, dtype=jnp.int32))
    return total

def reference(tokens, w_in, bias_in, w_out, bias_out, cotangent):
    preact = block_sum(tokens, w_in, 1, 0, N_COL) + bias_in
    value, slope = gelu_pair(preact)
    hidden = value.astype(jnp.bfloat16)
    outputs = (block_sum(hidden, w_out, 1, 0, N_ROW) + bias_out).astype(jnp.bfloat16)
    d_hidden = block_sum(cotangent, w_out, 1, 1, N_COL)
    d_preact = (d_hidden * slope).astype(jnp.bfloat16)
    grad_w_out = contract(hidden, cotangent, 0, 0).astype(jnp.bfloat16)
    grad_bias_out = lax.optimization_barrier(jnp.sum(cotangent.astype(jnp.float32), axis=0))
    grad_w_in = contract(tokens, d_preact, 0, 0).astype(jnp.bfloat16)
    grad_bias_in = lax.optimization_barrier(jnp.sum(d_preact.astype(jnp.float32), axis=0))
    d_tokens = block_sum(d_preact, w_in, 1, 1, N_ROW).astype(jnp.bfloat16)
    return (outputs, d_tokens, grad_w_in, grad_bias_in, grad_w_out, grad_bias_out)
```

```python
import math
from types import SimpleNamespace

import jax
import jax.numpy as jnp
from jax import lax
from jax.experimental import pallas as pl
from jax.experimental.pallas import tpu as pltpu
from jax.sharding import PartitionSpec as P

MESH = pl.DeviceIdType.MESH
BF, F32 = jnp.bfloat16, jnp.float32
NZ, NY, NX = 8, 4, 4
SHARD, DW, FW = 32, 1536, 768
CHUNK = 64
CA = 640
CB = DW - CA
POS = (0, 1, 4, 5, 7, 6, 3, 2)
SLOT = (0, 1, 7, 6, 2, 3, 5, 4)
ARRIVAL = (0, 1, 7, 2, 6, 3, 5, 4)
ZP, ZM, YP, YM, XP, XM, ZP2, ZM2, Y2, X2, CORE, LOCAL = range(12)
LINKS = ((ZP,), (ZM,), (YP,), (YM,), (XP,), (XM,), (ZP, ZP), (ZM, ZM), (YP, YM), (XP, XM), (), ())
QUICK, BRIEF, DIRECT = (True, False), (True, True), (True, True)
RATE, RATE_CORE, RATE_LOCAL = 44000.0, 600e3, 2.5e6
HOP, HOP_CORE, EACH = 2.6, 1.5, 0.03
RANK = (0.2, 0.2, 0.2, 0, 0.3, 0.3, 0.3, 0.3, 1.0, 0.665, 0.7, 0.045, 2.409, 0.627, 1.7, 1.61, 2.842, 2.7, 2.091, 2.7, 2.69, 4.014, 3.491, 5.647, 5.352, 5.527, 7.485, 9)
AHEAD = (1.5, 1.5, 1.5, 0.5, 0.0, 0.0, 0.0, 1.5, 2, 1.0, 5, 0.0, 0.5, 0.5, 0.5, 0.5, 0.2, 0.5, 0.5, 0.5, 1.5, 0.2, 1.0, 1.0, 1.0, 0.2, 0.2, 1)
EPS = 0.2
HALVES = ((0, 1), (0, 1))
gelu_coef = math.sqrt(2.0 / math.pi)


def gelu_pair(preact):
    inner = gelu_coef * (preact + 0.044715 * preact * preact * preact)
    tangent = jnp.tanh(inner)
    value = 0.5 * preact * (1.0 + tangent)
    slope = 0.5 * (1.0 + tangent) + 0.5 * preact * (1.0 - tangent * tangent) * gelu_coef * (
        1.0 + 3.0 * 0.044715 * preact * preact
    )
    return value, slope


def contract(left, right, left_dim, right_dim):
    return lax.dot_general(
        left, right, (((left_dim,), (right_dim,)), ((), ())), preferred_element_type=F32
    )


class Copy:
    def __init__(self, way, src, dst, size, land=None):
        self.way, self.src, self.dst, self.size = way, src, dst, size
        self.land = land or dst
        self.index = self.due = None
        self.then = []


class Task:
    def __init__(self, group, needs=(), after=(), run=None, cost=0.01, starts=(), minor=0.0):
        self.prio, self.ahead, self.group = RANK[group] + minor, AHEAD[group], group
        self.needs, self.after = list(needs), list(after)
        self.run, self.cost, self.starts = run, cost, list(starts)
        self.then = []


def arrange(tasks, log=None):
    now, free, order, left = 0.0, [0.0] * 12, [], list(tasks)
    for t in left:
        t.wait = len(set(t.after)) + len(set(t.needs))
        for one in set(t.after) | set(t.needs):
            one.then.append(t)
    able = [t for t in left if t.wait == 0]
    while able:
        best = None
        for place, t in enumerate(able):
            ready = max([now] + [n.due for n in t.needs])
            for c in t.starts:
                for link in LINKS[c.way]:
                    ready = max(ready, free[link] - t.ahead)
            key = (0.0 if ready <= now + EPS else ready, t.prio, place)
            if best is None or key < best[0]:
                best = (key, t)
        t = best[1]
        able.remove(t)
        begin = max([now] + [n.due for n in t.needs])
        if log is not None:
            log.append((begin, begin - now, t))
        now = begin + t.cost + EACH
        for c in t.starts:
            now += EACH
            if c.way >= CORE:
                free[c.way] = max(now, free[c.way]) + c.size / (RATE_CORE if c.way == CORE else RATE_LOCAL)
                c.due = free[c.way] + HOP_CORE
                continue
            c.due = 0.0
            for link in LINKS[c.way]:
                free[link] = max(now, free[link]) + c.size / RATE
                c.due = max(c.due, free[link] + HOP + (0.5 if c.way >= ZP2 else 0.0))
        order.append(t)
        for one in [t] + t.starts:
            for later in one.then:
                later.wait -= 1
                if later.wait == 0:
                    able.append(later)
    return order


def plan(r, at):
    copies, tasks = [], []

    def copy(way, src, dst, size, land=None):
        c = Copy(way, src, dst, size, land)
        c.index = len(copies)
        copies.append(c)
        return c

    def task(*args, **kw):
        t = Task(*args, **kw)
        tasks.append(t)
        return t

    def send(group, needs, way, src, dst, size, land=None, **kw):
        c = copy(way, src, dst, size, land)
        task(group, needs, starts=[c], **kw)
        return c

    A, B = slice(0, CA), slice(CA, DW)
    full, lo, hi = slice(0, SHARD), slice(0, 16), slice(16, 32)
    szA, szB = SHARD * CA * 2, SHARD * CB * 2

    def gather(arg, buf, quick, base):
        def ref(slot, *index):
            return lambda: buf().at[(POS[slot],) + index]

        def own(cols):
            return lambda: arg().at[:, cols]

        load = copy(LOCAL, arg, ref(0, 0), SHARD * DW * 2)
        whole = [[] for _ in range(NZ)]
        whole[0].append(load)
        yp0 = send(base, [], YP, own(A), ref(0, 2, full, A), szA)
        ym0 = send(base, [], YM, own(A), ref(0, 1, full, A), szA)
        zp = [send(base + 2, [], ZP, own(B), ref(7, 0, full, B), szB)]
        zm = [send(base + 2, [], ZM, own(B), ref(1, 0, full, B), szB)]
        task(base, starts=[load])
        y2 = send(base, [], Y2, own(A), ref(0, 3, full, A), szA)
        whole[0] += [yp0, ym0, y2]
        for s, need in enumerate(([], [ym0], [yp0], [y2])):
            for way in (ZP, ZM):
                got = need
                for k in range(4):
                    if k == 3 and (s < 2) != (way == ZP):
                        continue
                    here, there = ((8 - k) % 8, 7 - k) if way == ZP else (k, k + 1)
                    src = own(A) if k == 0 and s == 0 else ref(here, s, full, A)
                    got = [send(base + 1, got, way, src, ref(there, s, full, A), szA, minor=0.001 * k)]
                    whole[there] += got
        if quick:
            zp.append(send(base + 2, [], ZP2, own(B), ref(6, 0, full, B), szB))
            zm.append(send(base + 2, [], ZM2, own(B), ref(2, 0, full, B), szB))
            zp.append(send(base + 2, zp[1:], ZP, ref(6, 0, full, B), ref(5, 0, full, B), szB))
            zm.append(send(base + 2, zm[1:], ZM, ref(2, 0, full, B), ref(3, 0, full, B), szB))
            zp.append(send(base + 2, zp[1:2], ZP2, ref(6, 0, lo, B), ref(4, 0, lo, B), szB // 2))
            zm.append(send(base + 2, zm[1:2], ZM2, ref(2, 0, hi, B), ref(4, 0, hi, B), szB // 2))
        for k in range(1, 1 if quick else 4):
            rows, size = (lo, szB // 2) if k == 3 else (full, szB)
            zp.append(send(base + 2, zp[-1:], ZP, ref(8 - k, 0, rows, B), ref(7 - k, 0, rows, B), size))
            rows = hi if k == 3 else full
            zm.append(send(base + 2, zm[-1:], ZM, ref(k, 0, rows, B), ref(k + 1, 0, rows, B), size))
        column = [[load], zm[:1], zm[1:2], zm[2:3], [zp[3], zm[3]], zp[2:3], zp[1:2], zp[:1]]
        for i, slot in enumerate(ARRIVAL):
            src = own(B) if slot == 0 else ref(slot, 0, full, B)
            need = [] if slot == 0 else column[slot]
            p = send(base + 3, need, YP, src, ref(slot, 2, full, B), szB, minor=0.001 * i)
            m = send(base + 3, need, YM, src, ref(slot, 1, full, B), szB, minor=0.001 * i)
            if i % 2 == 0:
                last = send(base + 3, [p], YP, ref(slot, 2, full, B), ref(slot, 3, full, B), szB, minor=0.001 * i - 0.002)
            else:
                last = send(base + 3, [m], YM, ref(slot, 1, full, B), ref(slot, 3, full, B), szB, minor=0.001 * i - 0.002)
            whole[slot] += [p, m, last] + [c for c in column[slot] if c is not load]
        return whole

    tok = gather(lambda: r.tokens, lambda: r.T, QUICK[0], 0)
    load_in = copy(LOCAL, lambda: r.w_in, lambda: r.WI, DW * FW * 2)
    load_out = copy(LOCAL, lambda: r.w_out, lambda: r.WO, DW * FW * 2)
    load_bias_in = copy(LOCAL, lambda: r.bias_in, lambda: r.BI.at[0], FW * 4)
    load_bias_out = copy(LOCAL, lambda: r.bias_out, lambda: r.BO.at[0], DW * 4)
    task(0, starts=[load_in, load_out, load_bias_in, load_bias_out])
    cot = gather(lambda: r.cotangent, lambda: r.C, QUICK[1], 4)

    def reduce_col(buf, whole, weight, load, dim, s, total, finish, also, halves, direct, base):
        lo, hi = slice(0, 32), slice(32, 64)
        piece = 32 * FW * 2
        swaps = []

        def product(q, n):
            def run():
                left = buf()[2 * q : 2 * q + 2].reshape(256, DW)
                cols = slice(n * 256, n * 256 + 256)
                value = contract(left, weight()[:, cols], 1, 0) if dim == 0 else contract(left, weight()[cols, :], 1, 1)
                s().part[2 * q : 2 * q + 2, :, :, cols] = value.astype(BF).reshape(2, 2, CHUNK, 256)

            return run

        for q in [2 * h + i for h in halves for i in (0, 1)]:
            need = whole[SLOT[2 * q]] + whole[SLOT[2 * q + 1]] + [load]
            made = [task(base, need, run=product(q, n), cost=0.215) for n in range(3)]
            planes = slice(2 * q, 2 * q + 2)
            swaps.append(
                send(base + 1, [], CORE, lambda planes=planes: s().part.at[planes, at.other],
                     lambda planes=planes: s().swap.at[planes], 4 * piece, after=made)
            )
        ready = [None, None]
        for turn, h in enumerate(halves):
            swapped = swaps[2 * turn : 2 * turn + 2]

            def plane(rel, h=h):
                return 4 * h + at.x[rel]

            def add(rel, rows, extra=None, plane=plane, h=h):
                def run():
                    i = plane(rel)
                    value = s().part[i, at.core, rows, :].astype(F32) + s().swap[i, rows, :].astype(F32)
                    if extra is not None:
                        value = value + s().first[h, extra].astype(F32)
                    s().part[i, at.core, rows, :] = value.astype(BF)

                return run

            def part(rel, rows, plane=plane):
                return lambda: s().part.at[plane(rel), at.core, rows]

            def first(d, h=h):
                return lambda: s().first.at[h, d]

            def second(d, rows, h=h):
                return lambda: s().second.at[h, d, rows]

            u, v = base + 1, dict(minor=0.01 * turn)
            if direct:
                both = slice(0, CHUNK)
                p1 = send(u, swapped, XP, part(1, both), second(0, both), 2 * piece, run=add(1, both), cost=0.02, **v)
                m1 = send(u, swapped, XM, part(3, both), second(1, both), 2 * piece, run=add(3, both), cost=0.02, **v)
                p2 = m2 = send(u, swapped, X2, part(2, both), second(2, both), 2 * piece, run=add(2, both), cost=0.02, **v)
            else:
                p0 = send(u, swapped, XP, part(2, lo), first(0), piece, run=add(2, lo), cost=0.02, **v)
                m0 = send(u, swapped, XM, part(2, hi), first(1), piece, run=add(2, hi), cost=0.02, **v)
                p1 = send(u, swapped, XP, part(1, hi), second(0, hi), piece, run=add(1, hi), cost=0.02, **v)
                m1 = send(u, swapped, XM, part(3, lo), second(1, lo), piece, run=add(3, lo), cost=0.02, **v)
                p2 = send(u, swapped + [p0], XP, part(1, lo), second(0, lo), piece, run=add(1, lo, 0), cost=0.02, **v)
                m2 = send(u, swapped + [m0], XM, part(3, hi), second(1, hi), piece, run=add(3, hi, 1), cost=0.02, **v)

            def out(rel, core, rows, plane=plane):
                return lambda: total().at[plane(rel), getattr(at, core), rows]

            def final(at_row, plane=plane, h=h):
                def run():
                    @pl.loop(0, 2)
                    def _(n):
                        rows = pl.ds(pl.multiple_of(at_row + n * 16, 16), 16)
                        i = plane(0)
                        value = s().part[i, at.core, rows, :].astype(F32) + s().swap[i, rows, :].astype(F32)
                        for d in range(3 if direct else 2):
                            value = value + s().second[h, d, rows, :].astype(F32)
                        total()[i, at.core, rows, :] = finish(value, h, rows)

                return run

            me, ot = "core", "other"
            done, moved = [], {}
            for need, rows, at_row in (([p1, m2], hi, 32), ([p2, m1], lo, 0)):
                cp = copy(XP, out(0, me, rows), out(0, me, rows), piece, out(3, me, rows))
                cm = copy(XM, out(0, me, rows), out(0, me, rows), piece, out(1, me, rows))
                cs = copy(CORE, out(0, me, rows), out(0, me, rows), piece, out(0, ot, rows))
                starts = [cp, cm, cs]
                if direct:
                    need = [p1, m1, p2]
                    moved[2, at_row] = copy(X2, out(0, me, rows), out(0, me, rows), piece, out(2, me, rows))
                    starts.append(moved[2, at_row])
                task(base + 2, swapped + need + also, run=final(at_row), cost=0.17, starts=starts, **v)
                moved[3, at_row], moved[1, at_row] = cp, cm
                done.append(cs)
            for rel in (3, 1, 2) if direct else (3, 1):
                for rows, at_row in ((lo, 0), (hi, 32)):
                    c = moved[rel, at_row]
                    done += [c, send(base + 3, [c], CORE, out(rel, me, rows), out(rel, me, rows), piece, out(rel, ot, rows), **v)]
            for way, rel, rows, at_row in () if direct else ((XP, 3, lo, 0), (XM, 1, hi, 32)):
                c = send(base + 2, [moved[rel, at_row]], way, out(rel, me, rows), out(rel, me, rows), piece, out(2, me, rows), **v)
                done += [c, send(base + 3, [c], CORE, out(2, me, rows), out(2, me, rows), piece, out(2, ot, rows), **v)]
            ready[h] = done
        return ready

    def finish_hidden(value, h, rows):
        value, slope = gelu_pair(value + r.BI[...])
        r.slope[h, rows, :] = slope
        return value.astype(BF)

    def finish_d(value, h, rows):
        return (value * r.slope[h, rows, :]).astype(BF)

    hidden = reduce_col(
        lambda: r.T, tok, lambda: r.WI, load_in, 0, lambda: r.sum_h, lambda: r.H, finish_hidden, [load_bias_in], HALVES[0], DIRECT[0], 8)
    d_preact = reduce_col(
        lambda: r.C, cot, lambda: r.WO, load_out, 1, lambda: r.sum_d, lambda: r.D, finish_d, [], HALVES[1], DIRECT[1], 12)

    def reduce_row(total, ready, weight, dim, s, bias, also, target, brief, base):
        def product(q, n):
            def run():
                left = total()[2 * q : 2 * q + 2].reshape(256, FW)
                cols = slice(n * 512, n * 512 + 512)
                value = contract(left, weight()[:, cols], 1, 0) if dim == 0 else contract(left, weight()[cols, :], 1, 1)
                s().part[2 * q : 2 * q + 2, :, :, cols] = value.astype(BF).reshape(2, NY, SHARD, 512)

            return run

        made = {}
        for q in (0, 1, 3, 2):
            for n in range(3):
                made[q, n] = task(base, ready[q // 2], run=product(q, n), cost=0.215, minor=0.001 * n)

        def have(slot, cols):
            q = POS[slot] // 2
            return [made[q, n] for n in ((0, 1) if cols is A else (1, 2))]

        def ref(slot, *index):
            return lambda: s().part.at[(POS[slot],) + index]

        def add(slot, index, *sources):
            def run():
                place = (POS[slot],) + index
                value = s().part[place].astype(F32)
                for pick, at_place in sources:
                    value = value + pick(s())[at_place].astype(F32)
                s().part[place] = value.astype(BF)

            return run

        za, ya, yb, zb = (lambda t: t.za), (lambda t: t.ya), (lambda t: t.yb), (lambda t: t.zb)

        def buf(pick, *index):
            return lambda: pick(s()).at[index]

        own, got = {}, {}
        for s_ in (3, 1, 2, 0):
            ends = []
            for d, way in ((0, ZP), (1, ZM)):
                prev = None
                for k in range(4):
                    if k == 0 and (s_ < 2) != (way == ZP):
                        continue
                    slot = 4 - k if way == ZP else (4 + k) % 8
                    run = None if prev is None else add(slot, (s_, full, A), (za, (d, k - 1, s_)))
                    prev = send(base + 1, [prev] if prev else [], way, ref(slot, s_, full, A), buf(za, d, k, s_),
                                szA, minor=0.001 * (4 - k), after=have(slot, A), run=run, cost=0.02 if run else 0.01)
                ends.append(prev)
            own[s_] = task(base + 1, ends, have(0, A), run=add(0, (s_, full, A), (za, (0, 3, s_)), (za, (1, 3, s_))), cost=0.02)
        y2 = send(base + 2, [], Y2, ref(0, 3, full, A), buf(ya, 2), szA, after=[own[3]])
        p1 = send(base + 2, [], YP, ref(0, 1, full, A), buf(ya, 0), szA, after=[own[1]])
        m1 = send(base + 2, [], YM, ref(0, 2, full, A), buf(ya, 1), szA, after=[own[2]])
        summed = {}
        for i, slot in enumerate(reversed(ARRIVAL)):
            z = POS[slot]
            v = dict(minor=0.001 * i)
            d = i % 2
            here = have(slot, B)
            c0 = send(base + 3, [], (YP, YM)[d], ref(slot, 3, full, B), buf(yb, d, 0, z), szB, after=here, **v)
            ends = []
            for e, way in ((0, YP), (1, YM)):
                run = add(slot, (1 + e, full, B), (yb, (e, 0, z))) if e == d else None
                ends.append(send(base + 3, [c0] if run else [], way, ref(slot, 1 + e, full, B), buf(yb, e, 1, z), szB,
                                 after=here, run=run, cost=0.025 if run else 0.01, **v))
            summed[slot] = task(base + 3, ends, here, run=add(slot, (0, full, B), (yb, (0, 1, z)), (yb, (1, 1, z))), cost=0.03, **v)
        ends = []
        for d, way, way2 in ((0, ZP, ZP2), (1, ZM, ZM2)):
            prev = None
            half = (lo, hi)[d]
            if brief:
                far, near, mid, end = (4, 3, 2, 1) if way == ZP else (4, 5, 6, 7)
                b = base + 4
                c0 = send(b, [], way2, ref(far, 0, half, B), buf(zb, d, 0, half), szB // 2, after=[summed[far]])
                c1 = send(b, [], way, ref(near, 0, full, B), buf(zb, d, 1), szB, after=[summed[near]])
                c3 = send(b, [], way, ref(end, 0, full, B), buf(zb, d, 3), szB, after=[summed[end]])
                join = task(b, [c0, c1], [summed[mid]], run=add(mid, (0, full, B), (zb, (d, 1))), cost=0.02)
                c2 = send(b, [c0, c1], way2, ref(mid, 0, full, B), buf(zb, d, 2), szB, after=[join],
                          run=add(mid, (0, half, B), (zb, (d, 0, half))), cost=0.02)
                ends += [c2, c3]
                continue
            for k in range(4):
                slot = 4 - k if way == ZP else (4 + k) % 8
                rows, rows_in = (half if k == 0 else full), (half if k == 1 else full)
                run = None if prev is None else add(slot, (0, rows_in, B), (zb, (d, k - 1, rows_in)))
                prev = send(base + 4, [prev] if prev else [], way, ref(slot, 0, rows, B), buf(zb, d, k, rows),
                            szB // 2 if k == 0 else szB, after=[summed[slot]], run=run, cost=0.02 if run else 0.03)
            ends.append(prev)

        def last(cols, pick, places):
            def run():
                value = s().part[0, 0, :, cols].astype(F32)
                for place in places:
                    value = value + pick(s())[place].astype(F32)
                if bias is not None:
                    value = value + bias()[:, cols]
                target()[:, cols] = value.astype(BF)

            return run

        task(base + 2, [p1, m1, y2] + also, [own[0]], run=last(A, ya, (0, 1, 2)), cost=0.03)
        task(base + 4, ends + also, [summed[0]], run=last(B, zb, ((0, 3), (1, 3), (0, 2), (1, 2)) if brief else ((0, 3), (1, 3))), cost=0.03)

    reduce_row(lambda: r.H, hidden, lambda: r.WO, 0, lambda: r.sum_o, lambda: r.BO, [load_bias_out], lambda: r.outputs, BRIEF[0], 16)
    reduce_row(lambda: r.D, d_preact, lambda: r.WI, 1, lambda: r.sum_t, None, [], lambda: r.d_tokens, BRIEF[1], 21)

    all_tok, all_cot = sum(tok, []), sum(cot, [])

    def grad(left, right, target, i, wide):
        def run():
            cols = slice(i * 256, i * 256 + 256)
            a = left()[..., cols].reshape(1024, 256)
            target()[cols, :] = contract(a, right()[...].reshape(1024, wide), 0, 0).astype(BF)

        return run

    def column_sum(source, target):
        def run():
            whole = source()
            lead, width = whole.shape[1], whole.shape[-1]

            def step(n, total):
                return total + whole[n // lead, lax.rem(n, lead)].astype(F32)

            total = lax.fori_loop(0, NZ * lead, step, jnp.zeros(whole.shape[2:], F32))
            target()[...] = jnp.sum(total, axis=0, keepdims=True)

        return run

    for i in range(3):
        task(26, all_cot + sum(hidden, []), run=grad(lambda: r.H, lambda: r.C, lambda: r.grad_w_out, i, DW), cost=0.95)
    for i in range(6):
        task(26, all_tok + sum(d_preact, []), run=grad(lambda: r.T, lambda: r.D, lambda: r.grad_w_in, i, FW), cost=0.45)
    task(27, all_cot, run=column_sum(lambda: r.C, lambda: r.grad_bias_out), cost=0.75)
    task(27, sum(d_preact, []), run=column_sum(lambda: r.D, lambda: r.grad_bias_in), cost=0.4)
    return copies, tasks


def buffers():
    def v(*shape, dtype=BF):
        return pltpu.VMEM(shape, dtype)

    def col():
        return dict(part=v(NZ, 2, CHUNK, FW), swap=v(NZ, CHUNK, FW), first=v(2, 2, 32, FW), second=v(2, 3, CHUNK, FW))

    def row():
        return dict(part=v(NZ, NY, SHARD, DW), za=v(2, 4, NY, SHARD, CA), ya=v(3, SHARD, CA),
                    yb=v(2, 2, NZ, SHARD, CB), zb=v(2, 4, SHARD, CB))

    return dict(
        T=v(NZ, NY, SHARD, DW), C=v(NZ, NY, SHARD, DW), WI=v(DW, FW), WO=v(FW, DW),
        H=v(NZ, 2, CHUNK, FW), D=v(NZ, 2, CHUNK, FW), slope=v(2, CHUNK, FW, dtype=F32), BI=v(1, FW, dtype=F32), BO=v(1, DW, dtype=F32),
        sum_h=col(), sum_d=col(), sum_o=row(), sum_t=row(),
    )


def kernel(tokens, w_in, bias_in, w_out, bias_out, cotangent,
           outputs, d_tokens, grad_w_in, grad_bias_in, grad_w_out, grad_bias_out, scratch, send, recv):
    r = SimpleNamespace(**{k: SimpleNamespace(**b) if isinstance(b, dict) else b for k, b in scratch.items()})
    r.tokens, r.w_in, r.bias_in, r.w_out, r.bias_out, r.cotangent = tokens, w_in, bias_in, w_out, bias_out, cotangent
    r.outputs, r.d_tokens, r.grad_w_in, r.grad_bias_in = outputs, d_tokens, grad_w_in, grad_bias_in
    r.grad_w_out, r.grad_bias_out = grad_w_out, grad_bias_out
    row, col = lax.axis_index("row"), lax.axis_index("col")
    z, y, x, core = row // NY, lax.rem(row, NY), col // 2, lax.rem(col, 2)
    other = 1 - core
    xs = (x,) + tuple(lax.rem(x + d, NX) for d in (1, 2, 3))
    at = SimpleNamespace(x=xs, core=core, other=other)
    to = (
        (lax.rem(z + 1, NZ) * NY + y, col), (lax.rem(z + NZ - 1, NZ) * NY + y, col),
        (z * NY + lax.rem(y + 1, NY), col), (z * NY + lax.rem(y + NY - 1, NY), col),
        (row, xs[1] * 2 + core), (row, xs[3] * 2 + core),
        (lax.rem(z + 2, NZ) * NY + y, col), (lax.rem(z + NZ - 2, NZ) * NY + y, col),
        (z * NY + lax.rem(y + 2, NY), col), (row, xs[2] * 2 + core), (row, x * 2 + other),
    )
    barrier = pltpu.get_barrier_semaphore()
    for target in to:
        pl.semaphore_signal(barrier, inc=1, device_id=target, device_id_type=MESH)
    pl.semaphore_wait(barrier, len(to))

    def describe(c, dst):
        if c.way == LOCAL:
            return pltpu.make_async_copy(c.src(), dst(), recv.at[c.index])
        return pltpu.make_async_remote_copy(
            src_ref=c.src(), dst_ref=dst(), send_sem=send.at[c.index], recv_sem=recv.at[c.index],
            device_id=to[c.way], device_id_type=MESH,
        )

    copies, tasks = plan(r, at)
    waited = set()
    for t in arrange(tasks):
        for c in t.needs:
            if c.index not in waited:
                waited.add(c.index)
                if c.way == LOCAL:
                    describe(c, c.dst).wait()
                else:
                    describe(c, c.land).wait_recv()
        if t.run is not None:
            t.run()
        for c in t.starts:
            describe(c, c.dst).start()
    for c in copies:
        if c.way != LOCAL:
            describe(c, c.dst).wait_send()


def store_kernel(*refs):
    count = (len(refs) - 1) // 2
    moves = [
        pltpu.make_async_copy(refs[i] if len(refs[count + i].shape) == 2 else refs[i].at[0], refs[count + i], refs[-1].at[i])
        for i in range(count)
    ]
    for move in moves:
        move.start()
    for move in moves:
        move.wait()


def body(tokens, w_in, bias_in, w_out, bias_out, cotangent):
    any_space = pl.BlockSpec(memory_space=pl.ANY)
    vmem = pl.BlockSpec(memory_space=pltpu.VMEM)
    count = len(plan(None, None)[0])
    shapes = (((SHARD, DW), BF), ((SHARD, DW), BF), ((DW, FW), BF), ((1, FW), F32), ((FW, DW), BF), ((1, DW), F32))
    results = pl.pallas_call(
        kernel,
        out_shape=tuple(pltpu.VMEM(shape, dtype) for shape, dtype in shapes),
        in_specs=[any_space] * 6,
        out_specs=(vmem,) * 6,
        scratch_shapes=[buffers(), pltpu.SemaphoreType.DMA((count,)), pltpu.SemaphoreType.DMA((count,))],
        compiler_params=pltpu.CompilerParams(
            collective_id=0, has_side_effects=True, vmem_limit_bytes=52 << 20
        ),
        cost_estimate=pl.CostEstimate(
            flops=6 * 2 * 1024 * DW * FW, bytes_accessed=8 * DW * FW, transcendentals=128 * FW
        ),
        name="ffn",
    )(tokens, w_in, bias_in, w_out, bias_out, cotangent)
    results = pl.pallas_call(
        store_kernel,
        out_shape=tuple(jax.ShapeDtypeStruct(shape if shape[0] > 1 else shape[1:], dtype) for shape, dtype in shapes),
        in_specs=[any_space] * 6,
        out_specs=(any_space,) * 6,
        scratch_shapes=[pltpu.SemaphoreType.DMA((6,))],
        compiler_params=pltpu.CompilerParams(vmem_limit_bytes=1 << 20),
        name="store",
    )(*results)
    outputs, d_tokens, grad_w_in, grad_bias_in, grad_w_out, grad_bias_out = results
    return (outputs, d_tokens, grad_w_in, grad_bias_in, grad_w_out, grad_bias_out)


def solution(mesh):
    return jax.shard_map(
        body,
        mesh=mesh,
        in_specs=(
            P("row", "col"),
            P("col", "row"),
            P("row"),
            P("row", "col"),
            P("col"),
            P("row", "col"),
        ),
        out_specs=(
            P("row", "col"),
            P("row", "col"),
            P("col", "row"),
            P("row"),
            P("row", "col"),
            P("col"),
        ),
        check_vma=False,
    )
```

```python
import math
from types import SimpleNamespace

import jax
import jax.numpy as jnp
from jax import lax
from jax.experimental import pallas as pl
from jax.experimental.pallas import tpu as pltpu
from jax.sharding import PartitionSpec as P

MESH = pl.DeviceIdType.MESH
BF, F32 = jnp.bfloat16, jnp.float32
NZ, NY, NX = 8, 4, 4
SHARD, DW, FW = 32, 1536, 768
CHUNK = 64
CA = 640
CB = DW - CA
POS = (0, 1, 4, 5, 7, 6, 3, 2)
SLOT = (0, 1, 7, 6, 2, 3, 5, 4)
ARRIVAL = (0, 1, 7, 2, 6, 3, 5, 4)
ZP, ZM, YP, YM, XP, XM, CORE, LOCAL = range(8)
HALVES = ((0, 1), (0, 1))
ORDER = (2, 3, 0, 1, 67, 66, 68, 69, 11, 7, 41, 42, 24, 35, 36, 6, 5, 18, 14, 45, 47, 48, 102, 44, 21, 8, 111, 31,
    72, 37, 43, 65, 38, 25, 4, 12, 28, 46, 15, 50, 19, 53, 101, 51, 49, 117, 32, 71, 9, 39, 59, 54, 40, 22, 131, 57,
    26, 29, 56, 16, 104, 55, 103, 132, 52, 13, 63, 33, 133, 134, 10, 62, 90, 107, 58, 80, 61, 23, 60, 30, 20, 27, 17,
    64, 73, 123, 113, 34, 137, 136, 97, 119, 125, 122, 77, 135, 138, 116, 106, 94, 105, 141, 87, 126, 81, 118, 84,
    139, 148, 150, 140, 142, 147, 144, 143, 145, 146, 98, 74, 91, 114, 120, 149, 95, 164, 129, 163, 78, 70, 124, 166,
    88, 151, 85, 115, 165, 82, 121, 128, 99, 152, 75, 110, 92, 127, 168, 79, 96, 167, 89, 86, 154, 109, 83, 100, 130,
    183, 76, 93, 169, 108, 184, 112, 185, 186, 170, 153, 159, 188, 189, 187, 190, 155, 193, 192, 191, 194, 177, 175,
    212, 172, 211, 180, 181, 171, 161, 174, 179, 182, 214, 158, 160, 173, 156, 157, 213, 178, 176, 216, 196, 215,
    233, 234, 263, 242, 235, 275, 251, 247, 195, 277, 162, 258, 236, 237, 255, 238, 283, 239, 279, 267, 293, 217,
    291, 232, 218, 264, 197, 243, 231, 287, 200, 276, 248, 230, 252, 198, 229, 199, 256, 259, 285, 284, 225, 240,
    228, 268, 296, 281, 223, 265, 244, 303, 304, 227, 280, 278, 311, 307, 253, 201, 289, 288, 249, 257, 220, 202,
    292, 260, 219, 301, 221, 286, 222, 226, 224, 266, 269, 241, 295, 245, 323, 324, 337, 332, 325, 365, 348, 341,
    353, 369, 204, 209, 328, 207, 327, 373, 250, 326, 381, 357, 375, 329, 290, 367, 305, 203, 206, 409, 345, 419,
    333, 338, 294, 366, 261, 210, 308, 205, 246, 349, 354, 208, 370, 254, 371, 330, 282, 312, 374, 321, 322, 377,
    385, 320, 334, 299, 346, 378, 271, 318, 319, 270, 368, 401, 397, 389, 339, 342, 350, 272, 393, 358, 383, 262,
    410, 317, 382, 355, 416, 386, 331, 379, 297, 376, 335, 414, 372, 402, 398, 300, 420, 387, 347, 407, 309, 313,
    343, 412, 418, 411, 351, 340, 336, 362, 361, 391, 390, 384, 399, 380, 403, 421, 274, 359, 356, 395, 394, 298,
    314, 413, 302, 310, 344, 417, 352, 273, 363, 364, 388, 392, 400, 404, 415, 360, 315, 408, 306, 405, 316, 396,
    406)
gelu_coef = math.sqrt(2.0 / math.pi)


def gelu_pair(preact):
    inner = gelu_coef * (preact + 0.044715 * preact * preact * preact)
    tangent = jnp.tanh(inner)
    value = 0.5 * preact * (1.0 + tangent)
    slope = 0.5 * (1.0 + tangent) + 0.5 * preact * (1.0 - tangent * tangent) * gelu_coef * (
        1.0 + 3.0 * 0.044715 * preact * preact
    )
    return value, slope


def contract(left, right, left_dim, right_dim):
    return lax.dot_general(
        left, right, (((left_dim,), (right_dim,)), ((), ())), preferred_element_type=F32
    )


class Copy:
    def __init__(self, way, src, dst, size, land=None):
        self.way, self.src, self.dst, self.size = way, src, dst, size
        self.land = land or dst
        self.index = self.due = None
        self.then = []


class Task:
    def __init__(self, group, needs=(), after=(), run=None, cost=0.01, starts=(), minor=0.0):
        self.group, self.cost, self.minor = group, cost, minor
        self.needs, self.after, self.run, self.starts = list(needs), list(after), run, list(starts)


def plan(r, at):
    copies, tasks = [], []

    def copy(way, src, dst, size, land=None):
        c = Copy(way, src, dst, size, land)
        c.index = len(copies)
        copies.append(c)
        return c

    def task(*args, **kw):
        t = Task(*args, **kw)
        tasks.append(t)
        return t

    def send(group, needs, way, src, dst, size, land=None, **kw):
        c = copy(way, src, dst, size, land)
        task(group, needs, starts=[c], **kw)
        return c

    A, B = slice(0, CA), slice(CA, DW)
    full, lo, hi = slice(0, SHARD), slice(0, 16), slice(16, 32)
    szA, szB = SHARD * CA * 2, SHARD * CB * 2

    def gather(arg, buf, base):
        def ref(slot, *index):
            return lambda: buf().at[(POS[slot],) + index]

        def own(cols):
            return lambda: arg().at[:, cols]

        load = copy(LOCAL, arg, ref(0, 0), SHARD * DW * 2)
        whole = [[] for _ in range(NZ)]
        whole[0].append(load)
        yp0 = send(base, [], YP, own(A), ref(0, 2, full, A), szA)
        ym0 = send(base, [], YM, own(A), ref(0, 1, full, A), szA)
        zp = [send(base + 2, [], ZP, own(B), ref(7, 0, full, B), szB)]
        zm = [send(base + 2, [], ZM, own(B), ref(1, 0, full, B), szB)]
        task(base, starts=[load])
        yp1 = send(base, [yp0], YP, ref(0, 2, lo, A), ref(0, 3, lo, A), szA // 2)
        ym1 = send(base, [ym0], YM, ref(0, 1, hi, A), ref(0, 3, hi, A), szA // 2)
        whole[0] += [yp0, ym0, yp1, ym1]
        for s, need in enumerate(([], [ym0], [yp0], [yp1, ym1])):
            for way in (ZP, ZM):
                got = need
                for k in range(4):
                    if k == 3 and (s < 2) != (way == ZP):
                        continue
                    here, there = ((8 - k) % 8, 7 - k) if way == ZP else (k, k + 1)
                    src = own(A) if k == 0 and s == 0 else ref(here, s, full, A)
                    got = [send(base + 1, got, way, src, ref(there, s, full, A), szA, minor=0.001 * k)]
                    whole[there] += got
        for k in range(1, 4):
            rows, size = (lo, szB // 2) if k == 3 else (full, szB)
            zp.append(send(base + 2, zp[-1:], ZP, ref(8 - k, 0, rows, B), ref(7 - k, 0, rows, B), size))
            rows = hi if k == 3 else full
            zm.append(send(base + 2, zm[-1:], ZM, ref(k, 0, rows, B), ref(k + 1, 0, rows, B), size))
        column = [[load], zm[:1], zm[1:2], zm[2:3], [zp[3], zm[3]], zp[2:3], zp[1:2], zp[:1]]
        for i, slot in enumerate(ARRIVAL):
            src = own(B) if slot == 0 else ref(slot, 0, full, B)
            need = [] if slot == 0 else column[slot]
            p = send(base + 3, need, YP, src, ref(slot, 2, full, B), szB, minor=0.001 * i)
            m = send(base + 3, need, YM, src, ref(slot, 1, full, B), szB, minor=0.001 * i)
            if i % 2 == 0:
                last = send(base + 3, [p], YP, ref(slot, 2, full, B), ref(slot, 3, full, B), szB, minor=0.001 * i - 0.002)
            else:
                last = send(base + 3, [m], YM, ref(slot, 1, full, B), ref(slot, 3, full, B), szB, minor=0.001 * i - 0.002)
            whole[slot] += [p, m, last] + [c for c in column[slot] if c is not load]
        return whole

    tok = gather(lambda: r.tokens, lambda: r.T, 0)
    load_in = copy(LOCAL, lambda: r.w_in, lambda: r.WI, DW * FW * 2)
    load_out = copy(LOCAL, lambda: r.w_out, lambda: r.WO, DW * FW * 2)
    load_bias_in = copy(LOCAL, lambda: r.bias_in, lambda: r.BI.at[0], FW * 4)
    load_bias_out = copy(LOCAL, lambda: r.bias_out, lambda: r.BO.at[0], DW * 4)
    task(0, starts=[load_in, load_out, load_bias_in, load_bias_out])
    cot = gather(lambda: r.cotangent, lambda: r.C, 4)

    def reduce_col(buf, whole, weight, load, dim, s, total, finish, also, halves, base):
        lo, hi = slice(0, 32), slice(32, 64)
        piece = 32 * FW * 2
        swaps = []

        def product(q, n):
            def run():
                left = buf()[2 * q : 2 * q + 2].reshape(256, DW)
                cols = slice(n * 256, n * 256 + 256)
                value = contract(left, weight()[:, cols], 1, 0) if dim == 0 else contract(left, weight()[cols, :], 1, 1)
                s().part[2 * q : 2 * q + 2, :, :, cols] = value.astype(BF).reshape(2, 2, CHUNK, 256)

            return run

        for q in [2 * h + i for h in halves for i in (0, 1)]:
            need = whole[SLOT[2 * q]] + whole[SLOT[2 * q + 1]] + [load]
            made = [task(base, need, run=product(q, n), cost=0.215) for n in range(3)]
            planes = slice(2 * q, 2 * q + 2)
            swaps.append(
                send(base + 1, [], CORE, lambda planes=planes: s().part.at[planes, at.other],
                     lambda planes=planes: s().swap.at[planes], 4 * piece, after=made)
            )
        ready = [None, None]
        for turn, h in enumerate(halves):
            swapped = swaps[2 * turn : 2 * turn + 2]

            def plane(rel, h=h):
                return 4 * h + at.x[rel]

            def add(rel, rows, extra=None, plane=plane, h=h):
                def run():
                    i = plane(rel)
                    value = s().part[i, at.core, rows, :].astype(F32) + s().swap[i, rows, :].astype(F32)
                    if extra is not None:
                        value = value + s().first[h, extra].astype(F32)
                    s().part[i, at.core, rows, :] = value.astype(BF)

                return run

            def part(rel, rows, plane=plane):
                return lambda: s().part.at[plane(rel), at.core, rows]

            def first(d, h=h):
                return lambda: s().first.at[h, d]

            def second(d, rows, h=h):
                return lambda: s().second.at[h, d, rows]

            u, v = base + 1, dict(minor=0.01 * turn)
            p0 = send(u, swapped, XP, part(2, lo), first(0), piece, run=add(2, lo), cost=0.02, **v)
            m0 = send(u, swapped, XM, part(2, hi), first(1), piece, run=add(2, hi), cost=0.02, **v)
            p1 = send(u, swapped, XP, part(1, hi), second(0, hi), piece, run=add(1, hi), cost=0.02, **v)
            m1 = send(u, swapped, XM, part(3, lo), second(1, lo), piece, run=add(3, lo), cost=0.02, **v)
            p2 = send(u, swapped + [p0], XP, part(1, lo), second(0, lo), piece, run=add(1, lo, 0), cost=0.02, **v)
            m2 = send(u, swapped + [m0], XM, part(3, hi), second(1, hi), piece, run=add(3, hi, 1), cost=0.02, **v)

            def out(rel, core, rows, plane=plane):
                return lambda: total().at[plane(rel), getattr(at, core), rows]

            def final(at_row, plane=plane, h=h):
                def run():
                    @pl.loop(0, 2)
                    def _(n):
                        rows = pl.ds(pl.multiple_of(at_row + n * 16, 16), 16)
                        i = plane(0)
                        value = s().part[i, at.core, rows, :].astype(F32) + s().swap[i, rows, :].astype(F32)
                        for d in range(2):
                            value = value + s().second[h, d, rows, :].astype(F32)
                        total()[i, at.core, rows, :] = finish(value, h, rows)

                return run

            me, ot = "core", "other"
            done, moved = [], {}
            for need, rows, at_row in (([p1, m2], hi, 32), ([p2, m1], lo, 0)):
                cp = copy(XP, out(0, me, rows), out(0, me, rows), piece, out(3, me, rows))
                cm = copy(XM, out(0, me, rows), out(0, me, rows), piece, out(1, me, rows))
                cs = copy(CORE, out(0, me, rows), out(0, me, rows), piece, out(0, ot, rows))
                task(base + 2, swapped + need + also, run=final(at_row), cost=0.17, starts=[cp, cm, cs], **v)
                moved[3, at_row], moved[1, at_row] = cp, cm
                done.append(cs)
            for rel in (3, 1):
                for rows, at_row in ((lo, 0), (hi, 32)):
                    c = moved[rel, at_row]
                    done += [c, send(base + 3, [c], CORE, out(rel, me, rows), out(rel, me, rows), piece, out(rel, ot, rows), **v)]
            for way, rel, rows, at_row in ((XP, 3, lo, 0), (XM, 1, hi, 32)):
                c = send(base + 2, [moved[rel, at_row]], way, out(rel, me, rows), out(rel, me, rows), piece, out(2, me, rows), **v)
                done += [c, send(base + 3, [c], CORE, out(2, me, rows), out(2, me, rows), piece, out(2, ot, rows), **v)]
            ready[h] = done
        return ready

    def finish_hidden(value, h, rows):
        value, slope = gelu_pair(value + r.BI[...])
        r.slope[h, rows, :] = slope
        return value.astype(BF)

    def finish_d(value, h, rows):
        return (value * r.slope[h, rows, :]).astype(BF)

    hidden = reduce_col(
        lambda: r.T, tok, lambda: r.WI, load_in, 0, lambda: r.sum_h, lambda: r.H, finish_hidden, [load_bias_in], HALVES[0], 8)
    d_preact = reduce_col(
        lambda: r.C, cot, lambda: r.WO, load_out, 1, lambda: r.sum_d, lambda: r.D, finish_d, [], HALVES[1], 12)

    def reduce_row(total, ready, weight, dim, s, bias, also, target, base):
        def product(q, n):
            def run():
                left = total()[2 * q : 2 * q + 2].reshape(256, FW)
                cols = slice(n * 512, n * 512 + 512)
                value = contract(left, weight()[:, cols], 1, 0) if dim == 0 else contract(left, weight()[cols, :], 1, 1)
                s().part[2 * q : 2 * q + 2, :, :, cols] = value.astype(BF).reshape(2, NY, SHARD, 512)

            return run

        made = {}
        for q in (0, 1, 3, 2):
            for n in range(3):
                made[q, n] = task(base, ready[q // 2], run=product(q, n), cost=0.215, minor=0.001 * n)

        def have(slot, cols):
            q = POS[slot] // 2
            return [made[q, n] for n in ((0, 1) if cols is A else (1, 2))]

        def ref(slot, *index):
            return lambda: s().part.at[(POS[slot],) + index]

        def add(slot, index, *sources):
            def run():
                place = (POS[slot],) + index
                value = s().part[place].astype(F32)
                for pick, at_place in sources:
                    value = value + pick(s())[at_place].astype(F32)
                s().part[place] = value.astype(BF)

            return run

        za, ya, yb, zb = (lambda t: t.za), (lambda t: t.ya), (lambda t: t.yb), (lambda t: t.zb)

        def buf(pick, *index):
            return lambda: pick(s()).at[index]

        own, got = {}, {}
        for s_ in (3, 1, 2, 0):
            ends = []
            for d, way in ((0, ZP), (1, ZM)):
                prev = None
                for k in range(4):
                    if k == 0 and (s_ < 2) != (way == ZP):
                        continue
                    slot = 4 - k if way == ZP else (4 + k) % 8
                    run = None if prev is None else add(slot, (s_, full, A), (za, (d, k - 1, s_)))
                    prev = send(base + 1, [prev] if prev else [], way, ref(slot, s_, full, A), buf(za, d, k, s_),
                                szA, minor=0.001 * (4 - k), after=have(slot, A), run=run, cost=0.02 if run else 0.01)
                ends.append(prev)
            own[s_] = task(base + 1, ends, have(0, A), run=add(0, (s_, full, A), (za, (0, 3, s_)), (za, (1, 3, s_))), cost=0.02)
        p0 = send(base + 2, [], YP, ref(0, 3, lo, A), buf(ya, 0, 0, lo), szA // 2, after=[own[3]])
        m0 = send(base + 2, [], YM, ref(0, 3, hi, A), buf(ya, 1, 0, hi), szA // 2, after=[own[3]])
        p1 = send(base + 2, [p0], YP, ref(0, 1, full, A), buf(ya, 0, 1), szA, after=[own[1]],
                  run=add(0, (1, lo, A), (ya, (0, 0, lo))), cost=0.02)
        m1 = send(base + 2, [m0], YM, ref(0, 2, full, A), buf(ya, 1, 1), szA, after=[own[2]],
                  run=add(0, (2, hi, A), (ya, (1, 0, hi))), cost=0.02)
        summed = {}
        for i, slot in enumerate(reversed(ARRIVAL)):
            z = POS[slot]
            v = dict(minor=0.001 * i)
            d = i % 2
            here = have(slot, B)
            c0 = send(base + 3, [], (YP, YM)[d], ref(slot, 3, full, B), buf(yb, d, 0, z), szB, after=here, **v)
            ends = []
            for e, way in ((0, YP), (1, YM)):
                run = add(slot, (1 + e, full, B), (yb, (e, 0, z))) if e == d else None
                ends.append(send(base + 3, [c0] if run else [], way, ref(slot, 1 + e, full, B), buf(yb, e, 1, z), szB,
                                 after=here, run=run, cost=0.025 if run else 0.01, **v))
            summed[slot] = task(base + 3, ends, here, run=add(slot, (0, full, B), (yb, (0, 1, z)), (yb, (1, 1, z))), cost=0.03, **v)
        ends = []
        for d, way in ((0, ZP), (1, ZM)):
            prev = None
            half = (lo, hi)[d]
            for k in range(4):
                slot = 4 - k if way == ZP else (4 + k) % 8
                rows, rows_in = (half if k == 0 else full), (half if k == 1 else full)
                run = None if prev is None else add(slot, (0, rows_in, B), (zb, (d, k - 1, rows_in)))
                prev = send(base + 4, [prev] if prev else [], way, ref(slot, 0, rows, B), buf(zb, d, k, rows),
                            szB // 2 if k == 0 else szB, after=[summed[slot]], run=run, cost=0.02 if run else 0.03)
            ends.append(prev)

        def last(cols, pick, places):
            def run():
                value = s().part[0, 0, :, cols].astype(F32)
                for place in places:
                    value = value + pick(s())[place].astype(F32)
                if bias is not None:
                    value = value + bias()[:, cols]
                target()[:, cols] = value.astype(BF)

            return run

        task(base + 2, [p1, m1] + also, [own[0]], run=last(A, ya, ((0, 1), (1, 1))), cost=0.03)
        task(base + 4, ends + also, [summed[0]], run=last(B, zb, ((0, 3), (1, 3))), cost=0.03)

    reduce_row(lambda: r.H, hidden, lambda: r.WO, 0, lambda: r.sum_o, lambda: r.BO, [load_bias_out], lambda: r.outputs, 16)
    reduce_row(lambda: r.D, d_preact, lambda: r.WI, 1, lambda: r.sum_t, None, [], lambda: r.d_tokens, 21)

    all_tok, all_cot = sum(tok, []), sum(cot, [])

    def grad(left, right, target, i, n):
        def run():
            rows, cols = slice(i * 256, i * 256 + 256), slice(n * FW, n * FW + FW)
            a, b = left()[..., rows].reshape(1024, 256), right()[..., cols].reshape(1024, FW)
            target()[rows, cols] = contract(a, b, 0, 0).astype(BF)

        return run

    def column_sum(source, target, n):
        def run():
            cols = slice(n * FW, n * FW + FW)
            _, lead, rows, _ = source().shape

            def step(n, total):
                return total + source()[n // lead, lax.rem(n, lead), :, cols].astype(F32)

            total = lax.fori_loop(0, NZ * lead, step, jnp.zeros((rows, FW), F32))
            target()[:, cols] = jnp.sum(total, axis=0, keepdims=True)

        return run

    for i in range(6):
        task(26, all_cot + sum(hidden, []), run=grad(lambda: r.H, lambda: r.C, lambda: r.grad_w_out, i // 2, i % 2), cost=0.5)
    for i in range(6):
        task(26, all_tok + sum(d_preact, []), run=grad(lambda: r.T, lambda: r.D, lambda: r.grad_w_in, i, 0), cost=0.45)
    for n in range(2):
        task(27, all_cot, run=column_sum(lambda: r.C, lambda: r.grad_bias_out, n), cost=0.4)
    task(27, sum(d_preact, []), run=column_sum(lambda: r.D, lambda: r.grad_bias_in, 0), cost=0.4)
    return copies, tasks


def buffers():
    def v(*shape, dtype=BF):
        return pltpu.VMEM(shape, dtype)

    def col():
        return dict(part=v(NZ, 2, CHUNK, FW), swap=v(NZ, CHUNK, FW), first=v(2, 2, 32, FW), second=v(2, 2, CHUNK, FW))

    def row():
        return dict(part=v(NZ, NY, SHARD, DW), za=v(2, 4, NY, SHARD, CA), ya=v(2, 2, SHARD, CA),
                    yb=v(2, 2, NZ, SHARD, CB), zb=v(2, 4, SHARD, CB))

    return dict(
        T=v(NZ, NY, SHARD, DW), C=v(NZ, NY, SHARD, DW), WI=v(DW, FW), WO=v(FW, DW),
        H=v(NZ, 2, CHUNK, FW), D=v(NZ, 2, CHUNK, FW), slope=v(2, CHUNK, FW, dtype=F32), BI=v(1, FW, dtype=F32), BO=v(1, DW, dtype=F32),
        sum_h=col(), sum_d=col(), sum_o=row(), sum_t=row(),
    )


def kernel(tokens, w_in, bias_in, w_out, bias_out, cotangent,
           outputs, d_tokens, grad_w_in, grad_bias_in, grad_w_out, grad_bias_out, scratch, send, recv):
    r = SimpleNamespace(**{k: SimpleNamespace(**b) if isinstance(b, dict) else b for k, b in scratch.items()})
    r.tokens, r.w_in, r.bias_in, r.w_out, r.bias_out, r.cotangent = tokens, w_in, bias_in, w_out, bias_out, cotangent
    r.outputs, r.d_tokens, r.grad_w_in, r.grad_bias_in = outputs, d_tokens, grad_w_in, grad_bias_in
    r.grad_w_out, r.grad_bias_out = grad_w_out, grad_bias_out
    row, col = lax.axis_index("row"), lax.axis_index("col")
    z, y, x, core = row // NY, lax.rem(row, NY), col // 2, lax.rem(col, 2)
    other = 1 - core
    xs = (x,) + tuple(lax.rem(x + d, NX) for d in (1, 2, 3))
    at = SimpleNamespace(x=xs, core=core, other=other)
    to = (
        (lax.rem(z + 1, NZ) * NY + y, col), (lax.rem(z + NZ - 1, NZ) * NY + y, col),
        (z * NY + lax.rem(y + 1, NY), col), (z * NY + lax.rem(y + NY - 1, NY), col),
        (row, xs[1] * 2 + core), (row, xs[3] * 2 + core),
        (row, x * 2 + other),
    )
    barrier = pltpu.get_barrier_semaphore()
    for target in to:
        pl.semaphore_signal(barrier, inc=1, device_id=target, device_id_type=MESH)
    pl.semaphore_wait(barrier, len(to))

    def describe(c, dst):
        if c.way == LOCAL:
            return pltpu.make_async_copy(c.src(), dst(), recv.at[c.index])
        return pltpu.make_async_remote_copy(
            src_ref=c.src(), dst_ref=dst(), send_sem=send.at[c.index], recv_sem=recv.at[c.index],
            device_id=to[c.way], device_id_type=MESH,
        )

    copies, tasks = plan(r, at)
    waited = set()
    for t in (tasks[i] for i in ORDER):
        for c in t.needs:
            if c.index not in waited:
                waited.add(c.index)
                if c.way == LOCAL:
                    describe(c, c.dst).wait()
                else:
                    describe(c, c.land).wait_recv()
        if t.run is not None:
            t.run()
        for c in t.starts:
            describe(c, c.dst).start()
    for c in copies:
        if c.way != LOCAL:
            describe(c, c.dst).wait_send()


def store_kernel(*refs):
    count = (len(refs) - 1) // 2
    moves = [
        pltpu.make_async_copy(refs[i] if len(refs[count + i].shape) == 2 else refs[i].at[0], refs[count + i], refs[-1].at[i])
        for i in range(count)
    ]
    for move in moves:
        move.start()
    for move in moves:
        move.wait()


def body(tokens, w_in, bias_in, w_out, bias_out, cotangent):
    any_space = pl.BlockSpec(memory_space=pl.ANY)
    vmem = pl.BlockSpec(memory_space=pltpu.VMEM)
    count = len(plan(None, None)[0])
    shapes = (((SHARD, DW), BF), ((SHARD, DW), BF), ((DW, FW), BF), ((1, FW), F32), ((FW, DW), BF), ((1, DW), F32))
    results = pl.pallas_call(
        kernel,
        out_shape=tuple(pltpu.VMEM(shape, dtype) for shape, dtype in shapes),
        in_specs=[any_space] * 6,
        out_specs=(vmem,) * 6,
        scratch_shapes=[buffers(), pltpu.SemaphoreType.DMA((count,)), pltpu.SemaphoreType.DMA((count,))],
        compiler_params=pltpu.CompilerParams(
            collective_id=0, has_side_effects=True, vmem_limit_bytes=52 << 20
        ),
        cost_estimate=pl.CostEstimate(
            flops=6 * 2 * 1024 * DW * FW, bytes_accessed=8 * DW * FW, transcendentals=128 * FW
        ),
        name="ffn",
    )(tokens, w_in, bias_in, w_out, bias_out, cotangent)
    results = pl.pallas_call(
        store_kernel,
        out_shape=tuple(jax.ShapeDtypeStruct(shape if shape[0] > 1 else shape[1:], dtype) for shape, dtype in shapes),
        in_specs=[any_space] * 6,
        out_specs=(any_space,) * 6,
        scratch_shapes=[pltpu.SemaphoreType.DMA((6,))],
        compiler_params=pltpu.CompilerParams(vmem_limit_bytes=1 << 20),
        name="store",
    )(*results)
    outputs, d_tokens, grad_w_in, grad_bias_in, grad_w_out, grad_bias_out = results
    return (outputs, d_tokens, grad_w_in, grad_bias_in, grad_w_out, grad_bias_out)


def solution(mesh):
    return jax.shard_map(
        body,
        mesh=mesh,
        in_specs=(
            P("row", "col"),
            P("col", "row"),
            P("row"),
            P("row", "col"),
            P("col"),
            P("row", "col"),
        ),
        out_specs=(
            P("row", "col"),
            P("row", "col"),
            P("col", "row"),
            P("row"),
            P("row", "col"),
            P("col"),
        ),
        check_vma=False,
    )
```
